256 devices in a mesh: dp: 32 (over y, x, core), seq: 8 (over z).
Axes of the slice: x: 4, y: 4, z: 8, core: 2. Of those that a mesh axis runs over, the one named last changes fastest.
Arguments:
- t5_attn: bfloat16 [32, 128, 2048], P('dp', None, 'seq'), may hold values from -6 to 6
- t5_out_w: bfloat16 [2048, 4096], P('seq'), may hold values from -0.125 to 0.125
- t5_resid: bfloat16 [32, 128, 4096], P('dp', None, 'seq'), may hold values from -6 to 6
- text_dest: int32 [32, 128, 1], P('dp'), may hold values from 0 to 31; in each aligned block of 128 rows (0 to 127, 128 to 255, ..., all dimensions but the last counted through in order) at most 8 rows name the same one
- text_sample: int32 [32, 128], P('dp'), may hold values from 0 to 3
- kv_weight: bfloat16 [4096, 2, 2048], P(None, None, 'seq'), may hold values from -0.09375 to 0.09375
- img_query: bfloat16 [32, 2048, 2048], P('dp', 'seq'), may hold values from -32 to 32
- img_key: bfloat16 [32, 2048, 2048], P('dp', 'seq'), may hold values from -32 to 32
- img_value: bfloat16 [32, 2048, 2048], P('dp', 'seq'), may hold values from -6 to 6
- img_sample: int32 [32, 2048], P('dp'), may hold values from 0 to 3, never falling along the last dimension, each value on 1 to 1024 neighbouring positions
- proj_weight: bfloat16 [2048, 1536], P(('dp', 'seq')), may hold values from -0.125 to 0.125
- gate: float32 [32, 4, 1536], P('dp'), may hold values from -4 to 4
Outputs:
- block_out: bfloat16 [32, 2048, 1536], P('dp', 'seq')
The draws below stay inside these ranges and needn't reach their ends.
Inputs may be any that keep to these rules, and one draw needn't show every extreme that they name: `text_dest`: among the 128 text rows of one group at most 8 name the same destination group, and exactly 8 do so for some pair in every draw; every group is named by some row. `img_sample`: along a group's 2048 tokens the sample number never falls; every sample has 1 to 1024 tokens and one has exactly 1024.
All inputs are finite; a program needn't handle non-finite values.
Results may differ from the reference program's by a relative error of at most 0.018.
Values may be sent and summed in bfloat16 or wider, within the bound.
No kernel may reach another device: no remote copies, remote signals or barrier semaphores. Data moves between devices by JAX's collectives and lax.ppermute only.
A program may use at most 128 MiB of HBM per device.

```python
import math
import jax
import jax.numpy as jnp
import numpy as np
from jax import lax

T5_WIDTH = 4096
HEADS = 16
HEAD_DIM = 128
OUT_WIDTH = 1536
SAMPLES = 4
TEXT_GROUP = 128
T5_ATTN = 2048
ATTN_WIDTH = 2048
IMAGE_GROUP = 2048
CAPACITY = 8
N_DP = 32
N_SEQ = 8


def draw_img_query(key, part):
    key = jax.random.fold_in(key, 3)
    own_part = 1.5 * jnp.clip(jax.random.normal(key, (N_DP, IMAGE_GROUP, ATTN_WIDTH), jnp.float32), -6.0, 6.0)
    return own_part.astype(jnp.bfloat16)


def draw_img_key(key, part):
    key = jax.random.fold_in(key, 5)
    own_part = 1.5 * jnp.clip(jax.random.normal(key, (N_DP, IMAGE_GROUP, ATTN_WIDTH), jnp.float32), -6.0, 6.0)
    return own_part.astype(jnp.bfloat16)


def with_ends(array, own_key, least, top_value):
    longest = array.shape.index(max(array.shape))
    spots = []
    for shift in (0, 1):
        where = [jax.random.randint(jax.random.fold_in(own_key, axis), (), 0, length) for axis, length in enumerate(array.shape)]
        where[longest] = (where[longest] + shift) % array.shape[longest]
        spots.append(tuple(where))
    return array.at[spots[0]].set(least).at[spots[1]].set(top_value)


def block_levels(key, shape, shards, least, high):
    def one(dim, blocks):
        heights = jax.random.uniform(jax.random.fold_in(jax.random.fold_in(key, 6), dim), (blocks,), jnp.float32, least / len(shards), high / len(shards))
        return jnp.repeat(jnp.exp(heights), shape[dim] // blocks).reshape((-1,) + (1,) * (len(shape) - dim - 1))

    loudness = one(*shards[0])
    for cut in shards[1:]:
        loudness = loudness * one(*cut)
    return loudness


def length_profile(amount, total, reach, lean):
    portions = [(1 << 20) // math.isqrt(standing ** lean) + 1 for standing in range(2, amount + 1)]
    rest, given = total - reach - (amount - 1), [1] * (amount - 1)
    while rest > 0:
        candidates = [i for i in range(amount - 1) if given[i] < reach]
        mass, remaining = sum([portions[i] for i in candidates]), rest
        for i in candidates:
            extra = min(reach - given[i], max(1, remaining * portions[i] // mass), rest)
            given[i] = given[i] + extra
            rest = rest - extra
    return np.array([reach] + given)


def ragged_sizes(stream_key, count, total, most, skew):
    if count == 2:
        one = jax.random.randint(stream_key, (), max(1, total - most), min(most, total - 1) + 1)
        return jnp.stack([one, total - one])
    tallies = jnp.asarray(length_profile(count, total, most, skew), jnp.int32)
    couples = (count - 1) // 2
    source_of, taker = tallies[1:1 + 2 * couples:2], tallies[2:2 + 2 * couples:2]
    margin = jnp.minimum(source_of - 1, most - taker)
    passed = jax.random.randint(jax.random.fold_in(stream_key, 1), (couples,), 0, 1 << 20) % (margin + 1)
    tallies = tallies.at[1:1 + 2 * couples:2].set(source_of - passed).at[2:2 + 2 * couples:2].set(taker + passed)
    return tallies[jax.random.permutation(jax.random.fold_in(stream_key, 2), count)]


def deal_out(stream_key, own, number, rows, number_of, top, most, lean):
    ranking = jax.random.permutation(stream_key, number_of)
    heavy_load, ordinary = shares(number_of, rows * top, most, lean, True), shares(number_of, rows * top, most, lean, False)
    places = jnp.arange(number_of)

    def named(sizes, offset_by):
        used = int((sizes > 0).sum())
        fixed = max(1, used // 4)
        moved = fixed + (places - fixed + offset_by * (used - fixed)) % max(1, number_of - fixed)
        return jnp.zeros((number_of,), jnp.int32).at[ranking[jnp.where(places < fixed, places, moved)]].set(jnp.asarray(sizes, jnp.int32))

    sizes = jnp.where(number % 4 == 0, named(heavy_load, number // 4), named(ordinary, number - number // 4 - 1))
    mixed = jax.random.permutation(jax.random.fold_in(own, 3), number_of)
    giver, sink = mixed[0:number_of // 2 * 2:2], mixed[1:number_of // 2 * 2:2]
    margin = jnp.minimum(sizes[giver] - 1, most - sizes[sink]) // 2
    margin = jnp.where((giver == ranking[0]) | (sink == ranking[0]) | (sizes[sink] == 0), 0, jnp.maximum(margin, 0))
    moved = jax.random.randint(jax.random.fold_in(own, 4), (number_of // 2,), 0, 1 << 20) % (margin + 1)
    sizes = sizes.at[giver].add(-moved).at[sink].add(moved)
    labels = jnp.searchsorted(jnp.cumsum(sizes), jnp.arange(rows * top), side="right").astype(jnp.int32)
    table = labels.reshape(top, rows).T
    table = table[jax.random.permutation(jax.random.fold_in(own, 1), rows)]
    offset_by = jax.random.randint(jax.random.fold_in(own, 2), (rows, 1), 0, top)
    return jnp.take_along_axis(table, (jnp.arange(top)[None, :] + offset_by) % top, axis=1)


def shares(count, total, most, skew, full):
    portions = [(1 << 20) // math.isqrt(rank ** skew) + 1 for rank in range(1, count + 1)]
    largest = most if full else min(most, max(-(-total // count), total * portions[0] // sum(portions)))
    least = 1 if total - largest >= count - 1 else 0
    given, rest = [largest] + [least] * (count - 1), total - largest - least * (count - 1)
    while rest > 0:
        movable = [i for i in range(1, count) if given[i] < largest] or [i for i in range(1, count) if given[i] < most]
        pool, remaining = sum([portions[i] for i in movable]), rest
        for i in movable:
            addition = min(most - given[i], max(1, remaining * portions[i] // pool), rest)
            given[i] = given[i] + addition
            rest = rest - addition
    return np.array(given)


def gaussian(own_key, shape, width, reach, split=(), held_as=jnp.bfloat16):
    values = width * jax.random.normal(own_key, shape, jnp.float32)
    if split:
        values = values * block_levels(own_key, shape, split, -0.22, 0.18)
    return jnp.clip(values, -reach, reach).astype(held_as)


def setup_inputs(seed: int = 0) -> dict:
    streams_of = jax.random.split(jax.random.key(seed), 13)
    t5_attn = gaussian(streams_of[0], (N_DP, TEXT_GROUP, T5_ATTN), 1.0, 6.0, ((0, 32), (2, 8)))
    t5_out_w = gaussian(streams_of[1], (T5_ATTN, T5_WIDTH), T5_ATTN ** -0.5, 0.125, ((0, 8),))
    t5_resid = gaussian(streams_of[2], (N_DP, TEXT_GROUP, T5_WIDTH), 1.0, 6.0, ((0, 32), (2, 8)))
    text_dest_keys = jax.random.split(jax.random.fold_in(streams_of[3], 1), N_DP * TEXT_GROUP // TEXT_GROUP)
    text_dest_turns = jax.random.permutation(jax.random.fold_in(streams_of[3], 3), N_DP * TEXT_GROUP // TEXT_GROUP)
    text_dest = jax.vmap(lambda own, number: deal_out(jax.random.fold_in(streams_of[3], 2), own, number, TEXT_GROUP, N_DP, 1, CAPACITY, 2))(text_dest_keys, text_dest_turns).reshape((N_DP, TEXT_GROUP, 1))
    text_sample = with_ends(jax.random.randint(streams_of[4], (N_DP, TEXT_GROUP), 0, SAMPLES), jax.random.fold_in(streams_of[4], 1), 0, SAMPLES - 1).astype(jnp.int32)
    kv_weight = gaussian(streams_of[5], (T5_WIDTH, 2, ATTN_WIDTH), T5_WIDTH ** -0.5, 0.09375, ((2, 8),))
    img_query = draw_img_query(jax.random.fold_in(streams_of[12], 71), 0)
    img_key = draw_img_key(jax.random.fold_in(streams_of[12], 71), 0)
    img_value = gaussian(streams_of[8], (N_DP, IMAGE_GROUP, ATTN_WIDTH), 1.0, 6.0, ((0, 32), (1, 8)))
    img_sample = jax.vmap(lambda own: jnp.searchsorted(jnp.cumsum(ragged_sizes(own, SAMPLES, IMAGE_GROUP, IMAGE_GROUP // 2, 2)), jnp.arange(IMAGE_GROUP), side="right"))(jax.random.split(streams_of[9], N_DP)).reshape((N_DP, IMAGE_GROUP)).astype(jnp.int32)
    proj_weight = gaussian(streams_of[10], (ATTN_WIDTH, OUT_WIDTH), ATTN_WIDTH ** -0.5, 0.125, ((0, 256),))
    gate = gaussian(streams_of[11], (N_DP, SAMPLES, OUT_WIDTH), 1.0, 4.0, ((0, 32),), jnp.float32)
    return dict(t5_attn=t5_attn, t5_out_w=t5_out_w, t5_resid=t5_resid, text_dest=text_dest, text_sample=text_sample, kv_weight=kv_weight, img_query=img_query, img_key=img_key, img_value=img_value, img_sample=img_sample, proj_weight=proj_weight, gate=gate)


def reference(t5_attn, t5_out_w, t5_resid, text_dest, text_sample, kv_weight, img_query, img_key, img_value, img_sample, proj_weight, gate):
    head_block = T5_ATTN // N_SEQ
    feat_block = T5_WIDTH // N_SEQ
    summed = jnp.zeros((N_DP * TEXT_GROUP, T5_WIDTH), jnp.float32)
    for block_index in range(N_SEQ):
        attn_cols = t5_attn[:, :, block_index * head_block:(block_index + 1) * head_block].reshape(N_DP * TEXT_GROUP, head_block)
        partial_value = jnp.dot(attn_cols, t5_out_w[block_index * head_block:(block_index + 1) * head_block], preferred_element_type=jnp.float32)
        resid_cols = t5_resid[:, :, block_index * feat_block:(block_index + 1) * feat_block].reshape(N_DP * TEXT_GROUP, feat_block).astype(jnp.float32)
        partial_value = partial_value.at[:, block_index * feat_block:(block_index + 1) * feat_block].add(resid_cols)
        rounded = lax.optimization_barrier(partial_value.astype(jnp.bfloat16))
        summed = summed + rounded.astype(jnp.float32)
    t5_layer = summed.astype(jnp.bfloat16)
    projected_kv = jnp.dot(t5_layer, kv_weight.reshape(T5_WIDTH, 2 * ATTN_WIDTH), preferred_element_type=jnp.float32)
    key_part = projected_kv[:, :ATTN_WIDTH].reshape(-1, HEADS, HEAD_DIM)
    key_part = key_part * lax.rsqrt(lax.optimization_barrier(jnp.mean(key_part * key_part, axis=-1, keepdims=True)) + 1e-06)
    text_keys = key_part.astype(jnp.bfloat16)
    text_values = projected_kv[:, ATTN_WIDTH:].reshape(-1, HEADS, HEAD_DIM).astype(jnp.bfloat16)
    target = text_dest[:, :, 0].astype(jnp.int32)
    one_hot = (target[:, :, None] == jnp.arange(N_DP, dtype=jnp.int32)[None, None, :]).astype(jnp.int32)
    rank_of = lax.optimization_barrier(jnp.sum((jnp.cumsum(one_hot, axis=1).astype(jnp.int32) - one_hot) * one_hot, axis=2)).astype(jnp.int32)
    slot_of = target * CAPACITY + rank_of
    flat_slot = (jnp.arange(N_DP, dtype=jnp.int32)[:, None] * (N_DP * CAPACITY) + slot_of).reshape(-1)
    slot_table = jnp.full((N_DP * N_DP * CAPACITY,), -1, jnp.int32).at[flat_slot].set(jnp.arange(N_DP * TEXT_GROUP, dtype=jnp.int32))
    route_rows = jnp.transpose(slot_table.reshape(N_DP, N_DP, CAPACITY), (1, 0, 2)).reshape(N_DP, N_DP * CAPACITY)
    sample_flat = text_sample.reshape(-1).astype(jnp.int32)
    score_scale = 1.0 / math.sqrt(HEAD_DIM)

    def one_group(inputs):
        query_rows, key_image, value_image, sample, text_index = inputs
        filled = text_index >= 0
        safe_row = jnp.maximum(text_index, 0)
        key_sample = jnp.where(filled, sample_flat[safe_row], -1)
        all_keys = jnp.concatenate([key_image.reshape(-1, HEADS, HEAD_DIM), text_keys[safe_row]], axis=0).astype(jnp.float32)
        all_values = jnp.concatenate([value_image.reshape(-1, HEADS, HEAD_DIM), text_values[safe_row]], axis=0).astype(jnp.float32)
        queries = query_rows.reshape(-1, HEADS, HEAD_DIM).astype(jnp.float32)
        scores = jnp.einsum('qhd,khd->hqk', queries, all_keys) * score_scale
        allowed = sample[:, None] == jnp.concatenate([sample, key_sample])[None, :]
        scores = jnp.where(allowed[None], scores, -jnp.inf)
        largest = lax.optimization_barrier(jnp.max(scores, axis=-1, keepdims=True))
        exponent = jnp.exp(scores - largest)
        weights = (exponent / lax.optimization_barrier(jnp.sum(exponent, axis=-1, keepdims=True))).astype(jnp.bfloat16)
        attended = jnp.einsum('hqk,khd->qhd', weights.astype(jnp.float32), all_values)
        return attended.astype(jnp.bfloat16).reshape(IMAGE_GROUP, ATTN_WIDTH)
    attended = lax.map(one_group, (img_query, img_key, img_value, img_sample.astype(jnp.int32), route_rows))
    projected = jnp.dot(attended.reshape(-1, ATTN_WIDTH), proj_weight, preferred_element_type=jnp.float32).reshape(N_DP, IMAGE_GROUP, OUT_WIDTH)
    gate_rows = jax.vmap(lambda gate_group, sample_group: gate_group[sample_group])(gate, img_sample)
    return (gate_rows * projected).astype(jnp.bfloat16)
```

```python
import functools
import math

import jax
import jax.numpy as jnp
from jax import lax
from jax.experimental import pallas as pl
from jax.experimental.pallas import tpu as pltpu
from jax.sharding import PartitionSpec as P

HEAD_DIM = 128
PENALTY = 524288.0
CHUNK = 512
BF16 = jnp.bfloat16
F32 = jnp.float32
VMEM = pl.BlockSpec(memory_space=pltpu.VMEM)
SMEM = pl.BlockSpec(memory_space=pltpu.SMEM)
ANY = pl.BlockSpec(memory_space=pl.ANY)
PARAMS = pltpu.CompilerParams(vmem_limit_bytes=48 * 1024 * 1024)


def pack_kernel(lanes, lane_ref, q_ref, k_ref, v_ref, *refs):
    kv_out, q_out, sems = refs[:lanes], refs[lanes : 2 * lanes], refs[2 * lanes]
    width = q_ref.shape[1] // lanes
    copies = []
    for step in range(lanes):
        shift = (step + 4) % lanes
        owner = lax.rem(lane_ref[0] + shift, lanes)
        cols = pl.ds(pl.multiple_of(owner * width, width), width)
        copies.append(pltpu.make_async_copy(k_ref.at[:, cols], kv_out[shift].at[0], sems.at[3 * shift]))
        copies.append(pltpu.make_async_copy(v_ref.at[:, cols], kv_out[shift].at[1], sems.at[3 * shift + 1]))
        copies.append(pltpu.make_async_copy(q_ref.at[:, cols], q_out[shift], sems.at[3 * shift + 2]))
    for copy in copies:
        copy.start()
    for copy in copies:
        copy.wait()


def pack(lanes, lane, query, key, value):
    rows, features = query.shape
    width = features // lanes
    return pl.pallas_call(
        functools.partial(pack_kernel, lanes),
        out_shape=[jax.ShapeDtypeStruct((2, rows, width), BF16)] * lanes
        + [jax.ShapeDtypeStruct((rows, width), BF16)] * lanes,
        in_specs=[SMEM, ANY, ANY, ANY],
        out_specs=[ANY] * (2 * lanes),
        scratch_shapes=[pltpu.SemaphoreType.DMA((3 * lanes,))],
        name="pack",
    )(lane, query, key, value)


def text_kernel(steps, t5_ref, map_ref, kvw_ref, slot_ref, sample_ref, out_ref, total):
    step = pl.program_id(0)
    inner = map_ref.shape[0]

    @pl.when(step == 0)
    def _():
        total[...] = jnp.zeros_like(total)

    rows = t5_ref[0]
    total[...] += jnp.dot(rows[:, :inner], map_ref[...], preferred_element_type=F32) + jnp.dot(
        rows[:, inner:], kvw_ref[...], preferred_element_type=F32
    )

    @pl.when(step == steps - 1)
    def _():
        width = total.shape[1] // 2
        parts = []
        for head in range(width // HEAD_DIM):
            part = total[:, head * HEAD_DIM : (head + 1) * HEAD_DIM]
            part = part * lax.rsqrt(jnp.mean(part * part, axis=-1, keepdims=True) + 1e-06)
            parts.append(part.astype(BF16))
        parts.append(total[:, width:].astype(BF16))
        rows_kv = jnp.concatenate(parts, axis=1)
        slots, count = out_ref.shape[0], rows_kv.shape[0]
        taken = lax.broadcasted_iota(jnp.int32, (slots, count), 0) == slot_ref[...]
        chosen = taken.astype(F32).astype(BF16)
        out_ref[:, : 2 * width] = jnp.dot(chosen, rows_kv, preferred_element_type=F32).astype(BF16)
        slot_sample = jnp.sum(jnp.where(taken, sample_ref[...] + 1, 0), axis=1, keepdims=True) - 1
        column = lax.broadcasted_iota(jnp.int32, (slots, HEAD_DIM), 1)
        barred = (column < 4) & (column != slot_sample)
        out_ref[:, 2 * width :] = jnp.where(barred, -PENALTY, 0.0).astype(BF16)


def text_rows(t5_all, weight_map, kv_weight, slot_of, sample, slots):
    steps, count, both = t5_all.shape
    inner, width = weight_map.shape[0] // steps, weight_map.shape[1]
    return pl.pallas_call(
        functools.partial(text_kernel, steps),
        grid=(steps,),
        out_shape=jax.ShapeDtypeStruct((slots, width + HEAD_DIM), BF16),
        in_specs=[
            pl.BlockSpec((1, count, both), lambda i: (i, 0, 0)),
            pl.BlockSpec((inner, width), lambda i: (i, 0)),
            pl.BlockSpec((both - inner, width), lambda i: (i, 0)),
            pl.BlockSpec((1, count), lambda i: (0, 0)),
            pl.BlockSpec((1, count), lambda i: (0, 0)),
        ],
        out_specs=pl.BlockSpec((slots, width + HEAD_DIM), lambda i: (0, 0)),
        scratch_shapes=[pltpu.VMEM((count, width), F32)],
        compiler_params=PARAMS,
        name="text_rows",
    )(t5_all, weight_map, kv_weight, slot_of, sample)


def prepare_kernel(lanes, lane_ref, bar_ref, *refs):
    kv_refs, key_ref, value_ref = refs[:lanes], refs[lanes], refs[lanes + 1]
    rows = kv_refs[0].shape[1]
    heads = key_ref.shape[0]
    total = lanes * rows
    ones_rows = value_ref.shape[1] - HEAD_DIM
    column = lax.broadcasted_iota(jnp.int32, (rows, HEAD_DIM), 1)
    for head in range(heads):
        key_ref[head, total:, :HEAD_DIM] = jnp.zeros((rows, HEAD_DIM), BF16)
        key_ref[head, total:, HEAD_DIM:] = jnp.where(column < 4, -PENALTY, 0.0).astype(BF16)
        value_ref[head, :HEAD_DIM, total:] = jnp.zeros((HEAD_DIM, rows), BF16)
        value_ref[head, HEAD_DIM:, :] = jnp.ones((ones_rows, total + rows), BF16)
    for shift in range(lanes):
        source = lax.rem(lane_ref[0] + lanes - shift, lanes)
        place = pl.ds(pl.multiple_of(source * rows, rows), rows)
        for head in range(heads):
            cols = pl.ds(head * HEAD_DIM, HEAD_DIM)
            key_ref[head, place, :HEAD_DIM] = kv_refs[shift][0, :, cols]
            key_ref[head, place, HEAD_DIM:] = bar_ref[place, :]
            value = kv_refs[shift][1, :, cols].astype(F32)
            value_ref[head, :HEAD_DIM, place] = value.T.astype(BF16)


def prepare(lanes, lane, barred, kv_blocks):
    rows, width = kv_blocks[0].shape[1:]
    heads, total = width // HEAD_DIM, lanes * rows + rows
    return pl.pallas_call(
        functools.partial(prepare_kernel, lanes),
        out_shape=[
            jax.ShapeDtypeStruct((heads, total, 2 * HEAD_DIM), BF16),
            jax.ShapeDtypeStruct((heads, HEAD_DIM + 16, total), BF16),
        ],
        in_specs=[SMEM] + [VMEM] * (lanes + 1),
        out_specs=[VMEM, VMEM],
        compiler_params=PARAMS,
        name="prepare",
    )(lane, barred, *kv_blocks)


def attend_kernel(lanes, shifts, info_ref, hot_ref, text_ref, key_ref, value_ref, *refs):
    count = len(shifts)
    q_refs, out_refs = refs[:count], refs[count : 2 * count]
    q_all, out_all, text_key, text_value = refs[2 * count :]
    rows, width = q_refs[0].shape
    heads = width // HEAD_DIM
    exponent_scale = math.log2(math.e) / math.sqrt(HEAD_DIM)
    for index in range(count):
        q_all[index] = q_refs[index][...]
    for head in range(heads):
        cols = pl.ds(head * HEAD_DIM, HEAD_DIM)
        text_key[head, :, :HEAD_DIM] = text_ref[:, cols]
        text_key[head, :, HEAD_DIM:] = text_ref[:, 2 * width :]
        value = text_ref[:, pl.ds(width + head * HEAD_DIM, HEAD_DIM)].astype(F32)
        text_value[head, :HEAD_DIM] = value.T.astype(BF16)
        text_value[head, HEAD_DIM:] = jnp.ones_like(text_value[head, HEAD_DIM:])

    def block(index, carry):
        shift = info_ref[1 + 2 * lanes + index]
        source = lax.rem(info_ref[0] + lanes - shift, lanes)
        hot = hot_ref[pl.ds(pl.multiple_of(source * rows, rows), rows), :]
        queries = [
            jnp.concatenate([q_all[index, :, head * HEAD_DIM : (head + 1) * HEAD_DIM], hot], axis=1)
            for head in range(heads)
        ]

        def extend(head, keys, values, largest, total):
            scores = lax.dot_general(
                keys, queries[head], (((1,), (1,)), ((), ())), preferred_element_type=F32
            )
            bound = jnp.maximum(largest, jnp.max(scores, axis=0, keepdims=True))
            weights = jnp.exp2((scores - bound) * exponent_scale).astype(BF16)
            shrink = jnp.exp2((largest - bound) * exponent_scale)
            return bound, total * shrink + jnp.dot(values, weights, preferred_element_type=F32)

        state = []
        for head in range(heads):
            largest = jnp.full((1, rows), -1e30, F32)
            total = jnp.zeros((value_ref.shape[1], rows), F32)
            state.append(extend(head, text_key[head], text_value[head], largest, total))

        first = info_ref[1 + source]

        def chunk(number, state):
            place = pl.ds(pl.multiple_of(first + number * CHUNK, 256), CHUNK)
            return [
                extend(head, key_ref[head, place, :], value_ref[head, :, place], *state[head])
                for head in range(heads)
            ]

        state = lax.fori_loop(0, info_ref[1 + lanes + source], chunk, state)
        for head in range(heads):
            total = state[head][1]
            result = total[:HEAD_DIM] / total[HEAD_DIM : HEAD_DIM + 1]
            out_all[index, :, head * HEAD_DIM : (head + 1) * HEAD_DIM] = result.T.astype(BF16)
        return carry

    lax.fori_loop(0, count, block, 0)
    for index in range(count):
        out_refs[index][...] = out_all[index]


def attend(lanes, shifts, info, hot, text, keys, values, queries):
    rows, width = queries[0].shape
    heads, count = width // HEAD_DIM, len(shifts)
    info = jnp.concatenate([info, jnp.array(shifts, jnp.int32)])
    return pl.pallas_call(
        functools.partial(attend_kernel, lanes, shifts),
        out_shape=[jax.ShapeDtypeStruct((rows, width), BF16)] * count,
        in_specs=[SMEM] + [VMEM] * (4 + count),
        out_specs=[VMEM] * count,
        scratch_shapes=[
            pltpu.VMEM((count, rows, width), BF16),
            pltpu.VMEM((count, rows, width), BF16),
            pltpu.VMEM((heads, text.shape[0], 2 * HEAD_DIM), BF16),
            pltpu.VMEM((heads, values.shape[1], text.shape[0]), BF16),
        ],
        compiler_params=PARAMS,
        name="attend",
    )(info, hot, text, keys, values, *queries)


def project_kernel(lanes, lane_ref, weight_ref, gate_ref, *refs):
    blocks, out_ref = refs[:lanes], refs[lanes]
    depth = blocks[0].shape[1]
    total = jnp.zeros(out_ref.shape, F32)
    for shift in range(lanes):
        owner = lax.rem(lane_ref[0] + shift, lanes)
        part = weight_ref[pl.ds(pl.multiple_of(owner * depth, depth), depth), :]
        total += jnp.dot(blocks[shift][...], part, preferred_element_type=F32)
    out_ref[...] = (gate_ref[...] * total).astype(BF16)


def project(lanes, lane, weight, gate_rows, blocks):
    rows, width = gate_rows.shape
    depth, tile = weight.shape[0], width // 3
    return pl.pallas_call(
        functools.partial(project_kernel, lanes),
        grid=(3,),
        out_shape=jax.ShapeDtypeStruct((rows, width), BF16),
        in_specs=[
            SMEM,
            pl.BlockSpec((depth, tile), lambda i: (0, i)),
            pl.BlockSpec((rows, tile), lambda i: (0, i)),
        ]
        + [pl.BlockSpec(blocks[0].shape, lambda i: (0, 0))] * lanes,
        out_specs=pl.BlockSpec((rows, tile), lambda i: (0, i)),
        compiler_params=PARAMS,
        name="project",
    )(lane, weight, gate_rows, *blocks)


def on_device(
    t5_attn,
    t5_out_w,
    t5_resid,
    text_dest,
    text_sample,
    kv_weight,
    img_query,
    img_key,
    img_value,
    img_sample,
    proj_weight,
    gate,
):
    groups, lanes = lax.axis_size("dp"), lax.axis_size("seq")
    group, lane = lax.axis_index("dp"), lax.axis_index("seq")
    lane_ref = lane.reshape(1)
    text_count, inner = t5_attn.shape[1:]
    capacity = 2 * text_count // groups
    rows = img_query.shape[1]
    samples = gate.shape[1]

    def shifted(block, shift):
        return lax.ppermute(block, "seq", [(i, (i + shift) % lanes) for i in range(lanes)])

    t5_all = lax.all_gather(jnp.concatenate([t5_attn[0], t5_resid[0]], axis=1), "seq")
    share = inner // groups
    own_w = lax.dynamic_slice_in_dim(t5_out_w, group * share, share, 0)
    both = jnp.concatenate([own_w, proj_weight], axis=1)
    both = lax.all_to_all(jnp.broadcast_to(both[None], (lanes,) + both.shape), "seq", 0, 0)
    w_rows = both[:, :, : own_w.shape[1]].reshape(lanes * share, -1)
    proj_rows = both[:, :, own_w.shape[1] :].reshape(lanes * proj_weight.shape[0], -1)
    kv_flat = kv_weight.reshape(kv_weight.shape[0], -1)
    own_map = jnp.dot(w_rows, kv_flat, preferred_element_type=F32).astype(BF16)
    map_all = lax.all_to_all(jnp.broadcast_to(own_map[None], (groups,) + own_map.shape), "dp", 0, 0)
    map_all = map_all.reshape(groups, lanes, share, -1).transpose(1, 0, 2, 3).reshape(lanes * inner, -1)
    projection = lax.all_gather(proj_rows, "dp", axis=0, tiled=True)

    target = text_dest[0, :, 0]
    order = jnp.arange(text_count, dtype=jnp.int32)
    ahead = (target[None, :] == target[:, None]) & (order[:, None] < order[None, :])
    slot_of = target * capacity + jnp.sum(ahead.astype(jnp.int32), axis=0)

    sample = img_sample[0]
    column = jnp.arange(HEAD_DIM, dtype=jnp.int32)[None, :]
    hot = (sample[:, None] == column).astype(BF16)
    barred = jnp.where((column < samples) & (sample[:, None] != column), -PENALTY, 0.0).astype(BF16)
    ends = sample.reshape(lanes, rows)
    low = jnp.sum((sample[None, :] < ends[:, :1]).astype(jnp.int32), axis=1) // 256 * 256
    high = jnp.sum((sample[None, :] <= ends[:, -1:]).astype(jnp.int32), axis=1)
    info = jnp.concatenate([lane_ref, low, (high - low + CHUNK - 1) // CHUNK]).astype(jnp.int32)

    packed = pack(lanes, lane_ref, img_query[0], img_key[0], img_value[0])
    kv_out, q_out = packed[:lanes], packed[lanes:]
    order = (4, 3, 5, 2, 6, 1, 7)
    kv_in, q_in = {0: kv_out[0]}, {0: q_out[0]}
    for shift in order:
        kv_in[shift] = shifted(kv_out[shift], shift)
    for shift in order:
        q_in[shift] = shifted(q_out[shift], shift)

    sent = text_rows(t5_all, map_all, kv_flat, slot_of[None], text_sample, groups * capacity)
    text = lax.all_to_all(sent.reshape(groups, capacity, -1), "dp", 0, 0).reshape(sent.shape)

    keys, values = prepare(lanes, lane_ref, barred, [kv_in[s] for s in range(lanes)])
    returned = {}
    for shifts in SHIFT_GROUPS:
        results = attend(lanes, shifts, info, hot, text, keys, values, [q_in[s] for s in shifts])
        for shift, result in zip(shifts, results):
            returned[shift] = shifted(result, -shift) if shift else result

    own_sample = lax.dynamic_slice_in_dim(sample, lane * rows, rows)
    gate_rows = jnp.zeros((rows, gate.shape[2]), F32)
    for number in range(samples):
        gate_rows = jnp.where(own_sample[:, None] == number, gate[0, number][None, :], gate_rows)
    out = project(lanes, lane_ref, projection, gate_rows, [returned[s] for s in range(lanes)])
    return out[None]


SHIFT_GROUPS = ((4, 3, 5, 2, 6, 1, 7, 0),)


def solution(mesh):
    placed = (
        P("dp", None, "seq"),
        P("seq", None),
        P("dp", None, "seq"),
        P("dp", None, None),
        P("dp", None),
        P(None, None, "seq"),
        P("dp", "seq", None),
        P("dp", "seq", None),
        P("dp", "seq", None),
        P("dp", None),
        P(("dp", "seq"), None),
        P("dp", None, None),
    )
    return jax.shard_map(
        on_device, mesh=mesh, in_specs=placed, out_specs=P("dp", "seq", None), check_vma=False
    )
```

```python
import functools
import math

import jax
import jax.numpy as jnp
from jax import lax
from jax.experimental import pallas as pl
from jax.experimental.pallas import tpu as pltpu
from jax.sharding import PartitionSpec as P

HEAD_DIM = 128
PENALTY = 524288.0
CHUNK = 1024
ALIGN = 256
BF16 = jnp.bfloat16
F32 = jnp.float32
VMEM = pl.BlockSpec(memory_space=pltpu.VMEM)
SMEM = pl.BlockSpec(memory_space=pltpu.SMEM)
ANY = pl.BlockSpec(memory_space=pl.ANY)
PARAMS = pltpu.CompilerParams(vmem_limit_bytes=60 * 1024 * 1024)


def whole(array):
    zeros = (0,) * len(array.shape)
    return pl.BlockSpec(array.shape, lambda i: zeros)


def cost(microseconds):
    return pl.CostEstimate(flops=int(microseconds * 1.1e9), bytes_accessed=0, transcendentals=0)


def pack_kernel(lanes, lane_ref, *refs):
    sources = len(refs) - lanes
    width = refs[0].shape[1] // lanes
    for shift in range(lanes):
        owner = lax.rem(lane_ref[0] + shift, lanes)
        cols = pl.ds(pl.multiple_of(owner * width, width), width)
        for index in range(sources):
            refs[sources + shift][index] = refs[index][:, cols]


def pack(lanes, lane, *arrays):
    rows, features = arrays[0].shape
    out = jax.ShapeDtypeStruct((len(arrays), rows, features // lanes), arrays[0].dtype)
    return pl.pallas_call(
        functools.partial(pack_kernel, lanes),
        grid=(1,),
        out_shape=[out] * lanes,
        in_specs=[SMEM] + [whole(a) for a in arrays],
        out_specs=[whole(out)] * lanes,
        compiler_params=PARAMS,
        cost_estimate=cost(2),
        name="pack",
    )(lane, *arrays)


def text_kernel(steps, lane_ref, t5_ref, map_ref, kvw_ref, slot_ref, sample_ref, out_ref, total):
    step = pl.program_id(0)
    inner = map_ref.shape[0]

    @pl.when(step == 0)
    def _():
        total[...] = jnp.zeros_like(total)

    rows = t5_ref[0]
    total[...] += jnp.dot(rows[:, :inner], map_ref[...], preferred_element_type=F32) + jnp.dot(
        rows[:, inner:], kvw_ref[...], preferred_element_type=F32
    )

    @pl.when(step == steps - 1)
    def _():
        width = total.shape[1] // 2
        parts = []
        for head in range(width // HEAD_DIM):
            part = total[:, head * HEAD_DIM : (head + 1) * HEAD_DIM]
            part = part * lax.rsqrt(jnp.mean(part * part, axis=-1, keepdims=True) + 1e-06)
            parts.append(part.astype(BF16))
        parts.append(total[:, width:].astype(BF16))
        rows_kv = jnp.concatenate(parts, axis=1)
        slots, count = out_ref.shape[0], rows_kv.shape[0]
        taken = lax.broadcasted_iota(jnp.int32, (slots, count), 0) == slot_ref[...]
        chosen = taken.astype(F32).astype(BF16)
        out_ref[:, : 2 * width] = jnp.dot(chosen, rows_kv, preferred_element_type=F32).astype(BF16)
        slot_sample = jnp.sum(jnp.where(taken, sample_ref[...] + 1, 0), axis=1, keepdims=True) - 1
        column = lax.broadcasted_iota(jnp.int32, (slots, HEAD_DIM), 1)
        barred = (column < 4) & (column != slot_sample)
        out_ref[:, 2 * width :] = jnp.where(barred, -PENALTY, 0.0).astype(BF16)


def text_rows(lane, t5_all, weight_map, kv_weight, slot_of, sample, slots):
    steps, count, both = t5_all.shape
    inner, width = weight_map.shape[0] // steps, weight_map.shape[1]

    def source(i, lane_ref):
        return lax.rem(lane_ref[0] + steps - i, steps)

    return pl.pallas_call(
        functools.partial(text_kernel, steps),
        grid_spec=pltpu.PrefetchScalarGridSpec(
            num_scalar_prefetch=1,
            grid=(steps,),
            in_specs=[
                pl.BlockSpec((1, count, both), lambda i, lane_ref: (source(i, lane_ref), 0, 0)),
                pl.BlockSpec((inner, width), lambda i, lane_ref: (i, 0)),
                pl.BlockSpec((both - inner, width), lambda i, lane_ref: (source(i, lane_ref), 0)),
                pl.BlockSpec((1, count), lambda i, lane_ref: (0, 0)),
                pl.BlockSpec((1, count), lambda i, lane_ref: (0, 0)),
            ],
            out_specs=pl.BlockSpec((slots, width + HEAD_DIM), lambda i, lane_ref: (0, 0)),
            scratch_shapes=[pltpu.VMEM((count, width), F32)],
        ),
        out_shape=jax.ShapeDtypeStruct((slots, width + HEAD_DIM), BF16),
        compiler_params=PARAMS,
        cost_estimate=cost(5),
        name="text_rows",
    )(lane, t5_all, weight_map, kv_weight, slot_of, sample)


def prepare_kernel(lanes, lane_ref, bar_ref, *refs):
    kv_refs, key_ref, value_ref = refs[:lanes], refs[lanes], refs[lanes + 1]
    rows = kv_refs[0].shape[1]
    heads, _, extent = key_ref.shape
    total = lanes * rows
    feature = lax.broadcasted_iota(jnp.int32, (HEAD_DIM, extent - total), 0)
    for head in range(heads):
        key_ref[head, :HEAD_DIM, total:] = jnp.zeros((HEAD_DIM, extent - total), BF16)
        key_ref[head, HEAD_DIM:, total:] = jnp.where(feature < 4, -PENALTY, 0.0).astype(BF16)
        value_ref[head, total:, :HEAD_DIM] = jnp.zeros((extent - total, HEAD_DIM), BF16)
        value_ref[head, :, HEAD_DIM:] = jnp.ones((extent, HEAD_DIM), BF16)
    for shift in range(lanes):
        source = lax.rem(lane_ref[0] + lanes - shift, lanes)
        place = pl.ds(pl.multiple_of(source * rows, rows), rows)
        barred = bar_ref[place, :].astype(F32).T.astype(BF16)
        for head in range(heads):
            cols = pl.ds(head * HEAD_DIM, HEAD_DIM)
            key_ref[head, :HEAD_DIM, place] = kv_refs[shift][0, :, cols].astype(F32).T.astype(BF16)
            key_ref[head, HEAD_DIM:, place] = barred
            value_ref[head, place, :HEAD_DIM] = kv_refs[shift][1, :, cols]


def prepare(lanes, lane, barred, kv_blocks):
    rows, width = kv_blocks[0].shape[1:]
    heads, total = width // HEAD_DIM, lanes * rows + CHUNK - ALIGN
    outs = [
        jax.ShapeDtypeStruct((heads, 2 * HEAD_DIM, total), BF16),
        jax.ShapeDtypeStruct((heads, total, 2 * HEAD_DIM), BF16),
    ]
    return pl.pallas_call(
        functools.partial(prepare_kernel, lanes),
        grid=(1,),
        out_shape=outs,
        in_specs=[SMEM, whole(barred)] + [whole(block) for block in kv_blocks],
        out_specs=[whole(out) for out in outs],
        compiler_params=PARAMS,
        cost_estimate=cost(4),
        name="prepare",
    )(lane, barred, *kv_blocks)


def attend_kernel(lanes, shifts, info_ref, hot_ref, text_ref, key_ref, value_ref, *refs):
    count = len(shifts)
    q_refs, out_refs = refs[:count], refs[count : 2 * count]
    q_all, out_all, text_key, text_value = refs[2 * count :]
    rows, width = q_refs[0].shape[1:]
    heads = width // HEAD_DIM
    exponent_scale = math.log2(math.e) / math.sqrt(HEAD_DIM)
    for index in range(count):
        q_all[index] = q_refs[index][0]
    for head in range(heads):
        cols = pl.ds(head * HEAD_DIM, HEAD_DIM)
        text_key[head, :HEAD_DIM] = text_ref[:, cols].astype(F32).T.astype(BF16)
        text_key[head, HEAD_DIM:] = text_ref[:, 2 * width :].astype(F32).T.astype(BF16)
        text_value[head, :, :HEAD_DIM] = text_ref[:, pl.ds(width + head * HEAD_DIM, HEAD_DIM)]
        text_value[head, :, HEAD_DIM:] = jnp.ones_like(text_value[head, :, HEAD_DIM:])

    def block(index, carry):
        shift = info_ref[1 + 2 * lanes + index]
        source = lax.rem(info_ref[0] + lanes - shift, lanes)
        hot = hot_ref[pl.ds(pl.multiple_of(source * rows, rows), rows), :]
        queries = [
            jnp.concatenate([q_all[index, :, head * HEAD_DIM : (head + 1) * HEAD_DIM], hot], axis=1)
            for head in range(heads)
        ]

        def extend(keys, values, state):
            scores = [jnp.dot(queries[h], keys[h], preferred_element_type=F32) for h in range(heads)]
            bounds = [
                jnp.maximum(state[h][0], jnp.max(scores[h], axis=1, keepdims=True)) for h in range(heads)
            ]
            weights = [
                jnp.exp2((scores[h] - bounds[h]) * exponent_scale).astype(BF16) for h in range(heads)
            ]
            shrinks = [jnp.exp2((state[h][0] - bounds[h]) * exponent_scale) for h in range(heads)]
            return [
                (bounds[h], state[h][1] * shrinks[h] + jnp.dot(weights[h], values[h], preferred_element_type=F32))
                for h in range(heads)
            ]

        largest = jnp.full((rows, 1), -1e30, F32)
        total = jnp.zeros((rows, 2 * HEAD_DIM), F32)
        state = extend(
            [text_key[h] for h in range(heads)], [text_value[h] for h in range(heads)], [(largest, total)] * heads
        )
        first = info_ref[1 + source]

        def chunk(number, state):
            place = pl.ds(pl.multiple_of(first + number * CHUNK, ALIGN), CHUNK)
            return extend(
                [key_ref[h, :, place] for h in range(heads)], [value_ref[h, place, :] for h in range(heads)], state
            )

        state = lax.fori_loop(0, info_ref[1 + lanes + source], chunk, state)
        for head in range(heads):
            total = state[head][1]
            result = total[:, :HEAD_DIM] / total[:, HEAD_DIM:]
            out_all[index, :, head * HEAD_DIM : (head + 1) * HEAD_DIM] = result.astype(BF16)
        return carry

    lax.fori_loop(0, count, block, 0)
    for index in range(count):
        out_refs[index][...] = out_all[index]


def attend(lanes, shifts, info, hot, text, keys, values, queries):
    rows, width = queries[0].shape[1:]
    heads, count = width // HEAD_DIM, len(shifts)
    info = jnp.concatenate([info, jnp.array(shifts, jnp.int32)])
    out = jax.ShapeDtypeStruct((rows, width), BF16)
    return pl.pallas_call(
        functools.partial(attend_kernel, lanes, shifts),
        grid=(1,),
        out_shape=[out] * count,
        in_specs=[SMEM] + [whole(a) for a in (hot, text, keys, values, *queries)],
        out_specs=[whole(out)] * count,
        scratch_shapes=[
            pltpu.VMEM((count, rows, width), BF16),
            pltpu.VMEM((count, rows, width), BF16),
            pltpu.VMEM((heads, 2 * HEAD_DIM, text.shape[0]), BF16),
            pltpu.VMEM((heads, text.shape[0], 2 * HEAD_DIM), BF16),
        ],
        compiler_params=PARAMS,
        cost_estimate=cost(1 + 3 * count),
        name="attend",
    )(info, hot, text, keys, values, *queries)


def project_kernel(lanes, lane_ref, weight_ref, gate_ref, *refs):
    blocks, out_ref = refs[:lanes], refs[lanes]
    depth = blocks[0].shape[1]
    total = jnp.zeros(out_ref.shape, F32)
    for shift in range(lanes):
        owner = lax.rem(lane_ref[0] + shift, lanes)
        part = weight_ref[pl.ds(pl.multiple_of(owner * depth, depth), depth), :]
        total += jnp.dot(blocks[shift][...], part, preferred_element_type=F32)
    out_ref[...] = (gate_ref[...] * total).astype(BF16)


def project(lanes, lane, weight, gate_rows, blocks):
    rows, width = gate_rows.shape
    depth, tile = weight.shape[0], width // 3
    return pl.pallas_call(
        functools.partial(project_kernel, lanes),
        grid=(3,),
        out_shape=jax.ShapeDtypeStruct((rows, width), BF16),
        in_specs=[
            SMEM,
            pl.BlockSpec((depth, tile), lambda i: (0, i)),
            pl.BlockSpec((rows, tile), lambda i: (0, i)),
        ]
        + [pl.BlockSpec(blocks[0].shape, lambda i: (0, 0))] * lanes,
        out_specs=pl.BlockSpec((rows, tile), lambda i: (0, i)),
        compiler_params=PARAMS,
        cost_estimate=cost(5),
        name="project",
    )(lane, weight, gate_rows, *blocks)


def on_device(
    t5_attn,
    t5_out_w,
    t5_resid,
    text_dest,
    text_sample,
    kv_weight,
    img_query,
    img_key,
    img_value,
    img_sample,
    proj_weight,
    gate,
):
    groups, lanes = lax.axis_size("dp"), lax.axis_size("seq")
    group, lane = lax.axis_index("dp"), lax.axis_index("seq")
    lane_ref = lane.reshape(1)
    text_count, inner = t5_attn.shape[1:]
    capacity = 2 * text_count // groups
    rows = img_query.shape[1]
    samples = gate.shape[1]

    def shifted(block, shift):
        return lax.ppermute(block, "seq", [(i, (i + shift) % lanes) for i in range(lanes)])

    t5_all = lax.all_gather(jnp.concatenate([t5_attn[0], t5_resid[0]], axis=1), "seq")
    share = inner // groups
    own_w = lax.dynamic_slice_in_dim(t5_out_w, group * share, share, 0)
    both = jnp.concatenate([own_w, proj_weight], axis=1)
    shared = {0: both}
    for step in range(1, lanes // 2 + 1):
        shared[step] = shifted(shared[step - 1], 1)
        if step < lanes // 2:
            shared[lanes - step] = shifted(shared[(lanes - step + 1) % lanes], -1)
    w_rows = jnp.concatenate([shared[s][:, : own_w.shape[1]] for s in range(lanes)], axis=0)
    turned = [shared[s % lanes][:, own_w.shape[1] :] for s in range(lanes, -lanes, -1)]
    turned = jnp.concatenate(turned, axis=0)
    proj_count = proj_weight.shape[0]
    proj_rows = lax.dynamic_slice_in_dim(
        turned, (lanes - lane) * proj_count, lanes * proj_count, 0
    )
    kv_flat = kv_weight.reshape(kv_weight.shape[0], -1)
    own_map = jnp.dot(w_rows, kv_flat, preferred_element_type=F32).astype(BF16)
    map_all = lax.all_to_all(jnp.broadcast_to(own_map[None], (groups,) + own_map.shape), "dp", 0, 0)
    map_all = map_all.reshape(groups, lanes, share, -1).transpose(1, 0, 2, 3).reshape(lanes * inner, -1)
    projection = lax.all_gather(proj_rows, "dp", axis=0, tiled=True)

    target = text_dest[0, :, 0]
    order = jnp.arange(text_count, dtype=jnp.int32)
    ahead = (target[None, :] == target[:, None]) & (order[:, None] < order[None, :])
    slot_of = target * capacity + jnp.sum(ahead.astype(jnp.int32), axis=0)

    sample = img_sample[0]
    column = jnp.arange(HEAD_DIM, dtype=jnp.int32)[None, :]
    hot = (sample[:, None] == column).astype(BF16)
    barred = jnp.where((column < samples) & (sample[:, None] != column), -PENALTY, 0.0).astype(BF16)
    ends = sample.reshape(lanes, rows)
    low = jnp.sum((sample[None, :] < ends[:, :1]).astype(jnp.int32), axis=1) // ALIGN * ALIGN
    high = jnp.sum((sample[None, :] <= ends[:, -1:]).astype(jnp.int32), axis=1)
    info = jnp.concatenate([lane_ref, low, (high - low + CHUNK - 1) // CHUNK]).astype(jnp.int32)

    kv_out = pack(lanes, lane_ref, img_key[0], img_value[0])
    q_out = pack(lanes, lane_ref, img_query[0])
    kv_in, q_in = {0: kv_out[0]}, {0: q_out[0]}
    for shift in ORDER[:3]:
        kv_in[shift] = shifted(kv_out[shift], shift)
    kv_out, _ = lax.optimization_barrier((kv_out, [shared[3], shared[5]]))
    for shift in ORDER[3:]:
        kv_in[shift] = shifted(kv_out[shift], shift)
    q_out, _ = lax.optimization_barrier((q_out, [kv_in[s] for s in ORDER[:4]]))
    for shift in ORDER:
        q_in[shift] = shifted(q_out[shift], shift)

    sent = text_rows(lane_ref, t5_all, map_all, kv_flat, slot_of[None], text_sample, groups * capacity)
    text = lax.all_to_all(sent.reshape(groups, capacity, -1), "dp", 0, 0).reshape(sent.shape)

    keys, values = prepare(lanes, lane_ref, barred, [kv_in[s] for s in range(lanes)])
    returned = {}
    for shifts in SHIFT_GROUPS:
        results = attend(lanes, shifts, info, hot, text, keys, values, [q_in[s] for s in shifts])
        for shift, result in zip(shifts, results):
            returned[shift] = shifted(result, -shift) if shift else result

    own_sample = lax.dynamic_slice_in_dim(sample, lane * rows, rows)
    gate_rows = jnp.zeros((rows, gate.shape[2]), F32)
    for number in range(samples):
        gate_rows = jnp.where(own_sample[:, None] == number, gate[0, number][None, :], gate_rows)
    out = project(lanes, lane_ref, projection, gate_rows, [returned[s] for s in range(lanes)])
    return out[None]


ORDER = (4, 3, 5, 2, 6, 1, 7)
SHIFT_GROUPS = ((4, 3, 5), (2, 6, 1, 7), (0,))


def solution(mesh):
    placed = (
        P("dp", None, "seq"),
        P("seq", None),
        P("dp", None, "seq"),
        P("dp", None, None),
        P("dp", None),
        P(None, None, "seq"),
        P("dp", "seq", None),
        P("dp", "seq", None),
        P("dp", "seq", None),
        P("dp", None),
        P(("dp", "seq"), None),
        P("dp", None, None),
    )
    return jax.shard_map(
        on_device, mesh=mesh, in_specs=placed, out_specs=P("dp", "seq", None), check_vma=False
    )
```

```python
import functools
import math

import jax
import jax.numpy as jnp
from jax import lax
from jax.experimental import pallas as pl
from jax.experimental.pallas import tpu as pltpu
from jax.sharding import PartitionSpec as P

HEAD_DIM = 128
PENALTY = 524288.0
CHUNK = 1024
ALIGN = 256
BF16 = jnp.bfloat16
F32 = jnp.float32
VMEM = pl.BlockSpec(memory_space=pltpu.VMEM)
SMEM = pl.BlockSpec(memory_space=pltpu.SMEM)
ANY = pl.BlockSpec(memory_space=pl.ANY)
PARAMS = pltpu.CompilerParams(vmem_limit_bytes=60 * 1024 * 1024)


def whole(array):
    zeros = (0,) * len(array.shape)
    return pl.BlockSpec(array.shape, lambda i: zeros)


def cost(microseconds):
    return pl.CostEstimate(flops=int(microseconds * 1.1e9), bytes_accessed=0, transcendentals=0)


def pack_kernel(lanes, lane_ref, *refs):
    sources = len(refs) - lanes
    width = refs[0].shape[1] // lanes
    for shift in range(lanes):
        owner = lax.rem(lane_ref[0] + shift, lanes)
        cols = pl.ds(pl.multiple_of(owner * width, width), width)
        for index in range(sources):
            refs[sources + shift][index] = refs[index][:, cols]


def pack(lanes, lane, *arrays):
    rows, features = arrays[0].shape
    out = jax.ShapeDtypeStruct((len(arrays), rows, features // lanes), arrays[0].dtype)
    return pl.pallas_call(
        functools.partial(pack_kernel, lanes),
        grid=(1,),
        out_shape=[out] * lanes,
        in_specs=[SMEM] + [whole(a) for a in arrays],
        out_specs=[whole(out)] * lanes,
        compiler_params=PARAMS,
        cost_estimate=cost(2),
        name="pack",
    )(lane, *arrays)


def text_kernel(steps, lane_ref, t5_ref, map_ref, kvw_ref, slot_ref, sample_ref, out_ref, total):
    step = pl.program_id(0)
    inner = map_ref.shape[0]

    @pl.when(step == 0)
    def _():
        total[...] = jnp.zeros_like(total)

    rows = t5_ref[0]
    total[...] += jnp.dot(rows[:, :inner], map_ref[...], preferred_element_type=F32) + jnp.dot(
        rows[:, inner:], kvw_ref[...], preferred_element_type=F32
    )

    @pl.when(step == steps - 1)
    def _():
        width = total.shape[1] // 2
        parts = []
        for head in range(width // HEAD_DIM):
            part = total[:, head * HEAD_DIM : (head + 1) * HEAD_DIM]
            part = part * lax.rsqrt(jnp.mean(part * part, axis=-1, keepdims=True) + 1e-06)
            parts.append(part.astype(BF16))
        parts.append(total[:, width:].astype(BF16))
        rows_kv = jnp.concatenate(parts, axis=1)
        slots, count = out_ref.shape[0], rows_kv.shape[0]
        taken = lax.broadcasted_iota(jnp.int32, (slots, count), 0) == slot_ref[...]
        chosen = taken.astype(F32).astype(BF16)
        out_ref[:, : 2 * width] = jnp.dot(chosen, rows_kv, preferred_element_type=F32).astype(BF16)
        slot_sample = jnp.sum(jnp.where(taken, sample_ref[...] + 1, 0), axis=1, keepdims=True) - 1
        column = lax.broadcasted_iota(jnp.int32, (slots, HEAD_DIM), 1)
        barred = (column < 4) & (column != slot_sample)
        out_ref[:, 2 * width :] = jnp.where(barred, -PENALTY, 0.0).astype(BF16)


def text_rows(lane, t5_all, weight_map, kv_weight, slot_of, sample, slots):
    steps, count, both = t5_all.shape
    inner, width = weight_map.shape[0] // steps, weight_map.shape[1]

    def source(i, lane_ref):
        return lax.rem(lane_ref[0] + steps - i, steps)

    return pl.pallas_call(
        functools.partial(text_kernel, steps),
        grid_spec=pltpu.PrefetchScalarGridSpec(
            num_scalar_prefetch=1,
            grid=(steps,),
            in_specs=[
                pl.BlockSpec((1, count, both), lambda i, lane_ref: (source(i, lane_ref), 0, 0)),
                pl.BlockSpec((inner, width), lambda i, lane_ref: (i, 0)),
                pl.BlockSpec((both - inner, width), lambda i, lane_ref: (source(i, lane_ref), 0)),
                pl.BlockSpec((1, count), lambda i, lane_ref: (0, 0)),
                pl.BlockSpec((1, count), lambda i, lane_ref: (0, 0)),
            ],
            out_specs=pl.BlockSpec((slots, width + HEAD_DIM), lambda i, lane_ref: (0, 0)),
            scratch_shapes=[pltpu.VMEM((count, width), F32)],
        ),
        out_shape=jax.ShapeDtypeStruct((slots, width + HEAD_DIM), BF16),
        compiler_params=PARAMS,
        cost_estimate=cost(5),
        name="text_rows",
    )(lane, t5_all, weight_map, kv_weight, slot_of, sample)


def prepare_kernel(lanes, lane_ref, bar_ref, *refs):
    kv_refs, key_ref, value_ref = refs[:lanes], refs[lanes], refs[lanes + 1]
    rows = kv_refs[0].shape[1]
    heads, _, extent = key_ref.shape
    total = lanes * rows
    feature = lax.broadcasted_iota(jnp.int32, (HEAD_DIM, extent - total), 0)
    for head in range(heads):
        key_ref[head, :HEAD_DIM, total:] = jnp.zeros((HEAD_DIM, extent - total), BF16)
        key_ref[head, HEAD_DIM:, total:] = jnp.where(feature < 4, -PENALTY, 0.0).astype(BF16)
        value_ref[head, total:, :HEAD_DIM] = jnp.zeros((extent - total, HEAD_DIM), BF16)
        value_ref[head, :, HEAD_DIM:] = jnp.ones((extent, HEAD_DIM), BF16)
    for shift in range(lanes):
        source = lax.rem(lane_ref[0] + lanes - shift, lanes)
        place = pl.ds(pl.multiple_of(source * rows, rows), rows)
        barred = bar_ref[place, :].astype(F32).T.astype(BF16)
        for head in range(heads):
            cols = pl.ds(head * HEAD_DIM, HEAD_DIM)
            key_ref[head, :HEAD_DIM, place] = kv_refs[shift][0, :, cols].astype(F32).T.astype(BF16)
            key_ref[head, HEAD_DIM:, place] = barred
            value_ref[head, place, :HEAD_DIM] = kv_refs[shift][1, :, cols]


def prepare(lanes, lane, barred, kv_blocks):
    rows, width = kv_blocks[0].shape[1:]
    heads, total = width // HEAD_DIM, lanes * rows + CHUNK - ALIGN
    outs = [
        jax.ShapeDtypeStruct((heads, 2 * HEAD_DIM, total), BF16),
        jax.ShapeDtypeStruct((heads, total, 2 * HEAD_DIM), BF16),
    ]
    return pl.pallas_call(
        functools.partial(prepare_kernel, lanes),
        grid=(1,),
        out_shape=outs,
        in_specs=[SMEM, whole(barred)] + [whole(block) for block in kv_blocks],
        out_specs=[whole(out) for out in outs],
        compiler_params=PARAMS,
        cost_estimate=cost(4),
        name="prepare",
    )(lane, barred, *kv_blocks)


def attend_kernel(lanes, shifts, info_ref, hot_ref, text_ref, key_ref, value_ref, *refs):
    count = len(shifts)
    q_refs, out_refs = refs[:count], refs[count : 2 * count]
    q_all, out_all, text_key, text_value = refs[2 * count :]
    rows, width = q_refs[0].shape[1:]
    heads = width // HEAD_DIM
    exponent_scale = math.log2(math.e) / math.sqrt(HEAD_DIM)
    for index in range(count):
        q_all[index] = q_refs[index][0]
    for head in range(heads):
        cols = pl.ds(head * HEAD_DIM, HEAD_DIM)
        text_key[head, :HEAD_DIM] = text_ref[:, cols].astype(F32).T.astype(BF16)
        text_key[head, HEAD_DIM:] = text_ref[:, 2 * width :].astype(F32).T.astype(BF16)
        text_value[head, :, :HEAD_DIM] = text_ref[:, pl.ds(width + head * HEAD_DIM, HEAD_DIM)]
        text_value[head, :, HEAD_DIM:] = jnp.ones_like(text_value[head, :, HEAD_DIM:])

    def block(index, carry):
        shift = info_ref[1 + 2 * lanes + index]
        source = lax.rem(info_ref[0] + lanes - shift, lanes)
        hot = hot_ref[pl.ds(pl.multiple_of(source * rows, rows), rows), :]
        queries = [
            jnp.concatenate([q_all[index, :, head * HEAD_DIM : (head + 1) * HEAD_DIM], hot], axis=1)
            for head in range(heads)
        ]

        def extend(keys, values, state):
            scores = [jnp.dot(queries[h], keys[h], preferred_element_type=F32) for h in range(heads)]
            bounds = [
                jnp.maximum(state[h][0], jnp.max(scores[h], axis=1, keepdims=True)) for h in range(heads)
            ]
            weights = [
                jnp.exp2((scores[h] - bounds[h]) * exponent_scale).astype(BF16) for h in range(heads)
            ]
            shrinks = [jnp.exp2((state[h][0] - bounds[h]) * exponent_scale) for h in range(heads)]
            return [
                (bounds[h], state[h][1] * shrinks[h] + jnp.dot(weights[h], values[h], preferred_element_type=F32))
                for h in range(heads)
            ]

        largest = jnp.full((rows, 1), -1e30, F32)
        total = jnp.zeros((rows, 2 * HEAD_DIM), F32)
        state = extend(
            [text_key[h] for h in range(heads)], [text_value[h] for h in range(heads)], [(largest, total)] * heads
        )
        first = info_ref[1 + source]

        def chunk(number, state):
            place = pl.ds(pl.multiple_of(first + number * CHUNK, ALIGN), CHUNK)
            return extend(
                [key_ref[h, :, place] for h in range(heads)], [value_ref[h, place, :] for h in range(heads)], state
            )

        state = lax.fori_loop(0, info_ref[1 + lanes + source], chunk, state)
        for head in range(heads):
            total = state[head][1]
            result = total[:, :HEAD_DIM] / total[:, HEAD_DIM:]
            out_all[index, :, head * HEAD_DIM : (head + 1) * HEAD_DIM] = result.astype(BF16)
        return carry

    lax.fori_loop(0, count, block, 0)
    for index in range(count):
        out_refs[index][...] = out_all[index]


def attend(lanes, shifts, info, hot, text, keys, values, queries):
    rows, width = queries[0].shape[1:]
    heads, count = width // HEAD_DIM, len(shifts)
    info = jnp.concatenate([info, jnp.array(shifts, jnp.int32)])
    out = jax.ShapeDtypeStruct((rows, width), BF16)
    return pl.pallas_call(
        functools.partial(attend_kernel, lanes, shifts),
        grid=(1,),
        out_shape=[out] * count,
        in_specs=[SMEM] + [whole(a) for a in (hot, text, keys, values, *queries)],
        out_specs=[whole(out)] * count,
        scratch_shapes=[
            pltpu.VMEM((count, rows, width), BF16),
            pltpu.VMEM((count, rows, width), BF16),
            pltpu.VMEM((heads, 2 * HEAD_DIM, text.shape[0]), BF16),
            pltpu.VMEM((heads, text.shape[0], 2 * HEAD_DIM), BF16),
        ],
        compiler_params=PARAMS,
        cost_estimate=cost(1 + 3 * count),
        name="attend",
    )(info, hot, text, keys, values, *queries)


def project_kernel(lanes, lane_ref, weight_ref, gate_ref, *refs):
    blocks, out_ref = refs[:lanes], refs[lanes]
    depth = blocks[0].shape[1]
    total = jnp.zeros(out_ref.shape, F32)
    for shift in range(lanes):
        owner = lax.rem(lane_ref[0] + shift, lanes)
        part = weight_ref[pl.ds(pl.multiple_of(owner * depth, depth), depth), :]
        total += jnp.dot(blocks[shift][...], part, preferred_element_type=F32)
    out_ref[...] = (gate_ref[...] * total).astype(BF16)


def project(lanes, lane, weight, gate_rows, blocks):
    rows, width = gate_rows.shape
    depth, tile = weight.shape[0], width // 3
    return pl.pallas_call(
        functools.partial(project_kernel, lanes),
        grid=(3,),
        out_shape=jax.ShapeDtypeStruct((rows, width), BF16),
        in_specs=[
            SMEM,
            pl.BlockSpec((depth, tile), lambda i: (0, i)),
            pl.BlockSpec((rows, tile), lambda i: (0, i)),
        ]
        + [pl.BlockSpec(blocks[0].shape, lambda i: (0, 0))] * lanes,
        out_specs=pl.BlockSpec((rows, tile), lambda i: (0, i)),
        compiler_params=PARAMS,
        cost_estimate=cost(5),
        name="project",
    )(lane, weight, gate_rows, *blocks)


def on_device(
    t5_attn,
    t5_out_w,
    t5_resid,
    text_dest,
    text_sample,
    kv_weight,
    img_query,
    img_key,
    img_value,
    img_sample,
    proj_weight,
    gate,
):
    groups, lanes = lax.axis_size("dp"), lax.axis_size("seq")
    group, lane = lax.axis_index("dp"), lax.axis_index("seq")
    lane_ref = lane.reshape(1)
    text_count, inner = t5_attn.shape[1:]
    capacity = 2 * text_count // groups
    rows = img_query.shape[1]
    samples = gate.shape[1]

    def shifted(block, shift):
        return lax.ppermute(block, "seq", [(i, (i + shift) % lanes) for i in range(lanes)])

    t5_all = lax.all_gather(jnp.concatenate([t5_attn[0], t5_resid[0]], axis=1), "seq")
    share = inner // groups
    own_w = lax.dynamic_slice_in_dim(t5_out_w, group * share, share, 0)
    both = jnp.concatenate([own_w, proj_weight], axis=1)
    shared = {0: both}
    for step in range(1, lanes // 2 + 1):
        shared[step] = shifted(shared[step - 1], 1)
        if step < lanes // 2:
            shared[lanes - step] = shifted(shared[(lanes - step + 1) % lanes], -1)
    w_rows = jnp.concatenate([shared[s][:, : own_w.shape[1]] for s in range(lanes)], axis=0)
    turned = [shared[s % lanes][:, own_w.shape[1] :] for s in range(lanes, -lanes, -1)]
    turned = jnp.concatenate(turned, axis=0)
    proj_count = proj_weight.shape[0]
    proj_rows = lax.dynamic_slice_in_dim(
        turned, (lanes - lane) * proj_count, lanes * proj_count, 0
    )
    kv_flat = kv_weight.reshape(kv_weight.shape[0], -1)
    own_map = jnp.dot(w_rows, kv_flat, preferred_element_type=F32).astype(BF16)
    map_all = lax.all_to_all(jnp.broadcast_to(own_map[None], (groups,) + own_map.shape), "dp", 0, 0)
    map_all = map_all.reshape(groups, lanes, share, -1).transpose(1, 0, 2, 3).reshape(lanes * inner, -1)
    projection = lax.all_gather(proj_rows, "dp", axis=0, tiled=True)

    target = text_dest[0, :, 0]
    order = jnp.arange(text_count, dtype=jnp.int32)
    ahead = (target[None, :] == target[:, None]) & (order[:, None] < order[None, :])
    slot_of = target * capacity + jnp.sum(ahead.astype(jnp.int32), axis=0)

    sample = img_sample[0]
    column = jnp.arange(HEAD_DIM, dtype=jnp.int32)[None, :]
    hot = (sample[:, None] == column).astype(BF16)
    barred = jnp.where((column < samples) & (sample[:, None] != column), -PENALTY, 0.0).astype(BF16)
    ends = sample.reshape(lanes, rows)
    low = jnp.sum((sample[None, :] < ends[:, :1]).astype(jnp.int32), axis=1) // ALIGN * ALIGN
    high = jnp.sum((sample[None, :] <= ends[:, -1:]).astype(jnp.int32), axis=1)
    info = jnp.concatenate([lane_ref, low, (high - low + CHUNK - 1) // CHUNK]).astype(jnp.int32)

    kv_out = pack(lanes, lane_ref, img_key[0], img_value[0])
    q_out = pack(lanes, lane_ref, img_query[0])
    kv_in, q_in = {0: kv_out[0]}, {0: q_out[0]}
    for shift in NEAR:
        kv_in[shift] = shifted(kv_out[shift], shift)
    kv_out, _ = lax.optimization_barrier((kv_out, [shared[3], shared[5]]))
    for shift in FAR:
        kv_in[shift] = shifted(kv_out[shift], shift)
    q_out, _ = lax.optimization_barrier((q_out, [kv_in[s] for s in (*NEAR, FAR[0])]))
    for shift in ORDER:
        q_in[shift] = shifted(q_out[shift], shift)

    sent = text_rows(lane_ref, t5_all, map_all, kv_flat, slot_of[None], text_sample, groups * capacity)
    text = lax.all_to_all(sent.reshape(groups, capacity, -1), "dp", 0, 0).reshape(sent.shape)

    keys, values = prepare(lanes, lane_ref, barred, [kv_in[s] for s in range(lanes)])
    returned = {}
    for shifts in SHIFT_GROUPS:
        results = attend(lanes, shifts, info, hot, text, keys, values, [q_in[s] for s in shifts])
        for shift, result in zip(shifts, results):
            returned[shift] = shifted(result, -shift) if shift else result

    own_sample = lax.dynamic_slice_in_dim(sample, lane * rows, rows)
    gate_rows = jnp.zeros((rows, gate.shape[2]), F32)
    for number in range(samples):
        gate_rows = jnp.where(own_sample[:, None] == number, gate[0, number][None, :], gate_rows)
    out = project(lanes, lane_ref, projection, gate_rows, [returned[s] for s in range(lanes)])
    return out[None]


ORDER = (4, 3, 5, 2, 6, 1, 7)
NEAR, FAR = (1, 7, 2), (4, 3, 5, 6)
SHIFT_GROUPS = ((4, 3, 5), (2, 6, 1, 7), (0,))


def solution(mesh):
    placed = (
        P("dp", None, "seq"),
        P("seq", None),
        P("dp", None, "seq"),
        P("dp", None, None),
        P("dp", None),
        P(None, None, "seq"),
        P("dp", "seq", None),
        P("dp", "seq", None),
        P("dp", "seq", None),
        P("dp", None),
        P(("dp", "seq"), None),
        P("dp", None, None),
    )
    return jax.shard_map(
        on_device, mesh=mesh, in_specs=placed, out_specs=P("dp", "seq", None), check_vma=False
    )
```
